32 devices in a mesh: gx: 8 (over y, x, core), gy: 4 (over z).
Axes of the slice: x: 2, y: 2, z: 4, core: 2. Of those that a mesh axis runs over, the one named last changes fastest.
Arguments:
- e_field: float32 [3, 128, 32, 256], P(None, 'gx', 'gy'), may hold values from -6 to 6
- h_field: float32 [3, 128, 32, 256], P(None, 'gx', 'gy'), may hold values from -6 to 6
- currents: float32 [3, 128, 32, 256], P(None, 'gx', 'gy'), may hold values from -6 to 6
- material: int32 [128, 32, 256], P('gx', 'gy'), may hold values from 0 to 3
- coating: int32 [128, 32, 256], P('gx', 'gy'), may hold values 0 or 1
- mat_ca: float32 [4], replicated, may hold values from 0.4 to 1
- mat_cb: float32 [4], replicated, may hold values from 0.3 to 0.6
- drude: float32 [2], replicated, may hold values from 0.3 to 0.9
- inc_ez: float32 [4, 128], replicated, may hold values from -6 to 6
- inc_hy: float32 [4, 128], replicated, may hold values from -6 to 6
- box: int32 [6], replicated, may hold values from 1 to 254, as said below
Outputs:
- e_out: float32 [3, 128, 32, 256], P(None, 'gx', 'gy')
- h_out: float32 [3, 128, 32, 256], P(None, 'gx', 'gy')
- j_out: float32 [3, 128, 32, 256], P(None, 'gx', 'gy')
The draws below stay inside these ranges and needn't reach their ends.
Inputs may be any that keep to these rules, and one draw needn't show every extreme that they name: `box`: 1 <= x0 < 32 and 96 <= x1 <= 126; 1 <= y0 < 8 and 24 <= y1 <= 30; 1 <= z0 < 64 and 192 <= z1 <= 254; some lower bound is 1, and the upper bound along the longest dimension is that dimension's cells minus 2.
All inputs are finite; a program needn't handle non-finite values. No bound on the sum of `coating` on one device may be relied on, other than what follows from the above.
Results may differ from the reference program's by a relative error of at most 0.0001.
Values sent between devices are 32-bit elements; how exact they have to be, the bound alone decides.
A program may use at most 64 MiB of HBM per device.

```python
import jax
import jax.numpy as jnp

NZ = 256
STEPS = 4
NMAT = 4
NX = 128
NY = 32


def draw_box(key, part):
    key = jax.random.fold_in(key, 7)
    keys = jax.random.split(key, 7)
    extents = [NX, NY, NZ]
    longest = max(extents)
    chosen = jax.random.randint(keys[6], (), 0, 3)
    bounds = []
    for index, extent in enumerate(extents):
        lower = jax.random.randint(keys[2 * index], (), 1, max(extent // 4, 2))
        lower = jnp.where(chosen == index, 1, lower)
        upper = jax.random.randint(keys[2 * index + 1], (), 3 * extent // 4, extent - 1)
        if extent == longest:
            upper = jnp.zeros((), jnp.int32) + (extent - 2)
        bounds.append(lower.astype(jnp.int32))
        bounds.append(upper.astype(jnp.int32))
    return jnp.stack(bounds).astype(jnp.int32)


def set_ends(drawn, key, least, high):
    shape = drawn.shape
    spot = [jax.random.randint(jax.random.fold_in(key, axis), (), 0, shape[axis]) for axis in range(len(shape))]
    drawn = drawn.at[tuple(spot)].set(least)
    longest = shape.index(max(shape))
    spot[longest] = (spot[longest] + 1) % shape[longest]
    return drawn.at[tuple(spot)].set(high)


def levels(stream_key, dims, shards, least, largest):
    level = 1.0
    for position, blocks in shards:
        steps = jax.random.uniform(jax.random.fold_in(jax.random.fold_in(stream_key, 6), position), (blocks,), jnp.float32, least / len(shards), largest / len(shards))
        level = level * jnp.repeat(jnp.exp(steps), dims[position] // blocks).reshape((-1,) + (1,) * (len(dims) - 1 - position))
    return level


def bell_draw(own_key, shape, scale, most, shards=(), kind=jnp.bfloat16):
    array = scale * jax.random.normal(own_key, shape, jnp.float32)
    if shards:
        array = array * levels(own_key, shape, shards, -0.22, 0.18)
    return jnp.clip(array, -most, most).astype(kind)


def setup_inputs(seed: int = 0) -> dict:
    splits = jax.random.split(jax.random.key(seed), 12)
    e_field = bell_draw(splits[0], (3, NX, NY, NZ), 1.0, 6.0, ((1, 8), (2, 4)), jnp.float32)
    h_field = bell_draw(splits[1], (3, NX, NY, NZ), 1.0, 6.0, ((1, 8), (2, 4)), jnp.float32)
    currents = bell_draw(splits[2], (3, NX, NY, NZ), 1.0, 6.0, ((1, 8), (2, 4)), jnp.float32)
    material = set_ends(jax.random.randint(splits[3], (NX, NY, NZ), 0, NMAT), jax.random.fold_in(splits[3], 1), 0, NMAT - 1).astype(jnp.int32)
    coating = set_ends((jax.random.randint(splits[4], (NX, NY, NZ), 0, 3) < 1).astype(jnp.int32), jax.random.fold_in(splits[4], 1), 0, 1)
    mat_ca = jnp.clip(jax.random.uniform(splits[5], (NMAT,), jnp.float32, 0.4, 1.0), 0.4, 1.0)
    mat_cb = jnp.clip(jax.random.uniform(splits[6], (NMAT,), jnp.float32, 0.3, 0.6), 0.3, 0.6)
    drude = jnp.clip(jax.random.uniform(splits[7], (2,), jnp.float32, 0.3, 0.9), 0.3, 0.9)
    inc_ez = bell_draw(splits[8], (STEPS, NX), 1.0, 6.0, (), jnp.float32)
    inc_hy = bell_draw(splits[9], (STEPS, NX), 1.0, 6.0, (), jnp.float32)
    box = draw_box(jax.random.fold_in(splits[11], 71), 0)
    return dict(e_field=e_field, h_field=h_field, currents=currents, material=material, coating=coating, mat_ca=mat_ca, mat_cb=mat_cb, drude=drude, inc_ez=inc_ez, inc_hy=inc_hy, box=box)


CH = 0.5


def flag(cond):
    return cond.astype(jnp.float32)


def lookup(line, where_at):
    return jnp.sum(jnp.where(jnp.arange(line.shape[0], dtype=jnp.int32) == where_at, line, 0.0))


def h_sources(line, box, xi, yi, zi, local):
    wx = flag((xi >= box[0]) & (xi <= box[1]))
    wy = flag((yi >= box[2]) & (yi <= box[3]))
    wz = flag((zi >= box[4]) & (zi <= box[5]))
    fx = flag(xi == box[0] - 1) * (-lookup(line, box[0])) + flag(xi == box[1]) * lookup(line, box[1])
    dhy = CH * fx[:, None, None] * wy[None, :, None] * wz[None, None, :]
    fy = flag(yi == box[2] - 1) - flag(yi == box[3])
    dhx = CH * (local * wx)[:, None, None] * fy[None, :, None] * wz[None, None, :]
    return dhx, dhy


def e_sources(line, box, xi, yi, zi, local):
    wy = flag((yi >= box[2]) & (yi <= box[3]))
    wz = flag((zi >= box[4]) & (zi <= box[5]))
    fx = flag(xi == box[0]) * (-lookup(line, box[0] - 1)) + flag(xi == box[1]) * lookup(line, box[1])
    dez = fx[:, None, None] * wy[None, :, None] * wz[None, None, :]
    wopen = flag((xi >= box[0]) & (xi < box[1]))
    fz = flag(zi == box[4]) - flag(zi == box[5])
    dex = (local * wopen)[:, None, None] * wy[None, :, None] * fz[None, None, :]
    return dex, dez


def zfwd(field):
    return jnp.concatenate([field[:, :, 1:], jnp.zeros_like(field[:, :, :1])], 2) - field


def zbwd(field):
    return field - jnp.concatenate([jnp.zeros_like(field[:, :, :1]), field[:, :, :-1]], 2)


def curl_e(e, up_x, up_y):
    ex, ey, ez = e[0], e[1], e[2]
    dez_dx = jnp.concatenate([ez[1:], up_x[1]], 0) - ez
    dey_dx = jnp.concatenate([ey[1:], up_x[0]], 0) - ey
    dez_dy = jnp.concatenate([ez[:, 1:], up_y[1]], 1) - ez
    dex_dy = jnp.concatenate([ex[:, 1:], up_y[0]], 1) - ex
    return zfwd(ey) - dez_dy, dez_dx - zfwd(ex), dex_dy - dey_dx


def curl_h(h, low_x, low_y):
    hx, hy, hz = h[0], h[1], h[2]
    dhz_dy = hz - jnp.concatenate([low_y[1], hz[:, :-1]], 1)
    dhx_dy = hx - jnp.concatenate([low_y[0], hx[:, :-1]], 1)
    dhz_dx = hz - jnp.concatenate([low_x[1], hz[:-1]], 0)
    dhy_dx = hy - jnp.concatenate([low_x[0], hy[:-1]], 0)
    return dhz_dy - zbwd(hy), zbwd(hx) - dhz_dx, dhy_dx - dhx_dy


def reference(e_field, h_field, currents, material, coating, mat_ca, mat_cb, drude, inc_ez, inc_hy, box):
    ca = jnp.zeros(material.shape, jnp.float32)
    cb = jnp.zeros(material.shape, jnp.float32)
    for index in range(NMAT):
        ca = ca + flag(material == index) * mat_ca[index]
        cb = cb + flag(material == index) * mat_cb[index]
    coat = flag(coating == 1)
    width_x, width_y, depth = material.shape
    xi = jnp.arange(width_x, dtype=jnp.int32)
    yi = jnp.arange(width_y, dtype=jnp.int32)
    zi = jnp.arange(depth, dtype=jnp.int32)
    plane_x = jnp.zeros((2, 1, width_y, depth), jnp.float32)
    plane_y = jnp.zeros((2, width_x, 1, depth), jnp.float32)
    efield, hfield, jfield = e_field, h_field, currents
    for step in range(STEPS):
        curl_x, curl_y, curl_z = curl_e(efield, plane_x, plane_y)
        dhx, dhy = h_sources(inc_ez[step], box, xi, yi, zi, inc_ez[step])
        hfield = jnp.stack([hfield[0] + CH * curl_x + dhx, hfield[1] + CH * curl_y + dhy, hfield[2] + CH * curl_z])
        jfield = coat[None] * (drude[0] * jfield + drude[1] * efield)
        cur_x, cur_y, cur_z = curl_h(hfield, plane_x, plane_y)
        dex, dez = e_sources(inc_hy[step], box, xi, yi, zi, inc_hy[step])
        efield = jnp.stack([ca * efield[0] + cb * (cur_x + dex - jfield[0]), ca * efield[1] + cb * (cur_y - jfield[1]), ca * efield[2] + cb * (cur_z + dez - jfield[2])])
    return efield, hfield, jfield
```

```python
import functools

import jax
import jax.numpy as jnp
from jax import lax
from jax.experimental import pallas as pl
from jax.experimental.pallas import tpu as pltpu
from jax.sharding import PartitionSpec as P

CH = 0.5
MESH = pl.DeviceIdType.MESH

EX, EY, HX, HY, CEY, CEX = range(6)


def kernel(nx, ny, e_in, h_in, j_in, mat_in, coat_in, mat_ca, mat_cb, drude, inc_ez, inc_hy, box,
           e_out, h_out, j_out, E, H, J, M, C, CA, CB,
           s_ex, s_ey, s_hx, s_hy, s_cey, s_cex, r_ex, r_ey, r_hx, r_hy, r_cey, r_cex, low_y,
           load_sem, store_sem, send_sem, recv_sem):
    gx, gy = lax.axis_index("gx"), lax.axis_index("gy")
    steps = inc_ez.shape[0]
    wx, wy, depth = M.shape
    line_len = inc_ez.shape[1]

    loads = [pltpu.make_async_copy(src, dst, load_sem.at[i])
             for i, (src, dst) in enumerate([(mat_in, M), (coat_in, C), (e_in, E), (h_in, H), (j_in, J)])]
    for copy in loads:
        copy.start()

    has_lx, has_ux, has_ly, has_uy = gx > 0, gx < nx - 1, gy > 0, gy < ny - 1
    down_up, up_down = has_lx & has_uy, has_ux & has_ly
    to_lx, to_ux = (gx - 1, gy), (gx + 1, gy)
    to_ly, to_uy = (gx, gy - 1), (gx, gy + 1)
    to_du, to_ud = (gx - 1, gy + 1), (gx + 1, gy - 1)
    kinds = [
        (s_ex, r_ex, to_lx, has_lx, has_ux),
        (s_ey, r_ey, to_ly, has_ly, has_uy),
        (s_hx, r_hx, to_ux, has_ux, has_lx),
        (s_hy, r_hy, to_uy, has_uy, has_ly),
        (s_cey, r_cey, to_du, down_up, up_down),
        (s_cex, r_cex, to_ud, up_down, down_up),
    ]

    for _, dst, _, _, comes in kinds:
        @pl.when(jnp.logical_not(comes))
        def _():
            dst[...] = jnp.zeros_like(dst)

    barrier = pltpu.get_barrier_semaphore()
    for target, exists in [(to_lx, has_lx), (to_ux, has_ux), (to_ly, has_ly), (to_uy, has_uy),
                           (to_du, down_up), (to_ud, up_down)]:
        @pl.when(exists)
        def _():
            pl.semaphore_signal(barrier, inc=1, device_id=target, device_id_type=MESH)

    def copy_of(kind, step):
        src, dst, target, _, _ = kinds[kind]
        return pltpu.make_async_remote_copy(
            src_ref=src.at[step], dst_ref=dst.at[step], send_sem=send_sem.at[step, kind],
            recv_sem=recv_sem.at[step, kind], device_id=target, device_id_type=MESH)

    def send(kind, step):
        @pl.when(kinds[kind][3])
        def _():
            copy_of(kind, step).start()

    x0, x1, y0, y1, z0, z1 = [box[i] for i in range(6)]
    shape = (wy, depth)
    row = lax.broadcasted_iota(jnp.int32, shape, 0)
    lane = lax.broadcasted_iota(jnp.int32, shape, 1)
    yi = row + gy * wy
    first_row, last_row = row == 0, row == wy - 1
    first_lane, last_lane = lane == 0, lane == depth - 1
    in_y = (yi >= y0) & (yi <= y1)
    in_z = (lane >= z0) & (lane <= z1)
    f32 = lambda cond: jnp.where(cond, 1.0, 0.0).astype(jnp.float32)
    zero = jnp.zeros(shape, jnp.float32)
    w_yz = f32(in_y & in_z)
    fy_z = (f32(yi == y0 - 1) - f32(yi == y1)) * f32(in_z) * CH
    y_fz = f32(in_y) * (f32(lane == z0) - f32(lane == z1))
    start_x = gx * wx

    zup = lambda f: jnp.where(last_lane, zero, pltpu.roll(f, depth - 1, 1))
    zdn = lambda f: jnp.where(first_lane, zero, pltpu.roll(f, 1, 1))
    yup = lambda f: pltpu.roll(f, wy - 1, 0)
    ydn = lambda f: pltpu.roll(f, 1, 0)

    loads[0].wait()
    a = [mat_ca[i] for i in range(mat_ca.shape[0])]
    b = [mat_cb[i] for i in range(mat_cb.shape[0])]
    for x in range(wx):
        m = M[x]
        va, vb = jnp.full(shape, a[0], jnp.float32), jnp.full(shape, b[0], jnp.float32)
        for i in range(1, len(a)):
            va, vb = jnp.where(m == i, a[i], va), jnp.where(m == i, b[i], vb)
        CA[x], CB[x] = va, vb
    kd, bd = drude[0], drude[1]
    for copy in loads[1:]:
        copy.wait()
    pl.semaphore_wait(barrier, sum(jnp.where(c, 1, 0) for c in (has_lx, has_ux, has_ly, has_uy, down_up, up_down)))

    def one_step(step, carry):
        s_ex[step, 0], s_ex[step, 1] = E[1, 0], E[2, 0]
        send(EX, step)
        for x in range(wx):
            s_ey[step, 0, pl.ds(x, 1), :] = E[0, x, pl.ds(0, 1), :]
            s_ey[step, 1, pl.ds(x, 1), :] = E[2, x, pl.ds(0, 1), :]
        send(EY, step)
        s_cey[step] = E[1, 0, pl.ds(wy - 1, 1), :]
        send(CEY, step)
        s_cex[step] = E[0, wx - 1, pl.ds(0, 1), :]
        send(CEX, step)

        ez_x0, ez_x1 = inc_ez[step, x0], inc_ez[step, x1]
        for x in range(wx):
            xi = start_x + x
            ex, ey, ez = E[0, x], E[1, x], E[2, x]
            ey_up = E[1, x + 1] if x + 1 < wx else zero
            ez_up = E[2, x + 1] if x + 1 < wx else zero
            ez_y = jnp.where(last_row, zero, yup(ez))
            ex_y = jnp.where(last_row, zero, yup(ex))
            fx = CH * (jnp.where(xi == x1, ez_x1, 0.0) - jnp.where(xi == x0 - 1, ez_x0, 0.0))
            local = jnp.where((xi >= x0) & (xi <= x1), inc_ez[step, xi], 0.0)
            hx = H[0, x] + CH * ((zup(ey) - ey) - (ez_y - ez)) + local * fy_z
            hy = H[1, x] + CH * ((ez_up - ez) - (zup(ex) - ex)) + fx * w_yz
            hz = H[2, x] + CH * ((ex_y - ex) - (ey_up - ey))
            H[0, x], H[1, x], H[2, x] = hx, hy, hz
            s_hy[step, 0, pl.ds(x, 1), :] = hx[wy - 1:wy]
            s_hy[step, 1, pl.ds(x, 1), :] = hz[wy - 1:wy]
        send(HY, step)
        s_hx[step, 0], s_hx[step, 1] = H[1, wx - 1], H[2, wx - 1]
        send(HX, step)

        hy_x0, hy_x1 = inc_hy[step, jnp.maximum(x0 - 1, 0)], inc_hy[step, x1]
        for x in range(wx):
            xi = start_x + x
            fx = jnp.where(xi == x1, hy_x1, 0.0) - jnp.where(xi == x0, hy_x0, 0.0)
            local = jnp.where((xi >= x0) & (xi < x1), inc_hy[step, xi], 0.0)
            coat = C[x] == 1
            ca, cb = CA[x], CB[x]
            for c in range(3):
                e = E[c, x]
                j = jnp.where(coat, kd * J[c, x] + bd * e, zero)
                J[c, x] = j
                t = -j
                if c == 0:
                    t = local * y_fz - j
                if c == 2:
                    t = fx * w_yz - j
                E[c, x] = ca * e + cb * t

        @pl.when(step == steps - 1)
        def _():
            pltpu.make_async_copy(J, j_out, store_sem.at[2]).start()

        for kind in range(6):
            @pl.when(kinds[kind][4])
            def _():
                copy_of(kind, step).wait_recv()

        has_y = jnp.where(has_ly, 1.0, 0.0).astype(jnp.float32)
        has_x = jnp.where(has_lx, 1.0, 0.0).astype(jnp.float32)
        low_y[0] = has_y * (r_hy[step, 0] - CH * s_ey[step, 1])
        low_y[1] = has_y * (r_hy[step, 1] + CH * s_ey[step, 0])
        low_y[1, pl.ds(wx - 1, 1), :] = low_y[1, pl.ds(wx - 1, 1), :] - (CH * has_y) * r_cey[step]
        hy_low = has_x * (r_hx[step, 0] + CH * s_ex[step, 1])
        corner = jnp.where(last_row, jnp.broadcast_to(r_cex[step], shape), zero)
        hz_low = has_x * (r_hx[step, 1] - CH * (s_ex[step, 0] - corner))
        for x in range(wx):
            ez_up = jnp.broadcast_to(r_ey[step, 1, pl.ds(x, 1), :], shape)
            ex_up = jnp.broadcast_to(r_ey[step, 0, pl.ds(x, 1), :], shape)
            hx = H[0, x] - jnp.where(last_row, CH * ez_up, zero)
            hy = H[1, x]
            hz = H[2, x] + jnp.where(last_row, CH * ex_up, zero)
            if x == wx - 1:
                hy = hy + CH * r_ex[step, 1]
                hz = hz - CH * r_ex[step, 0]
                H[1, x] = hy
            H[0, x], H[2, x] = hx, hz
            cb = CB[x]
            hx_y = jnp.where(first_row, jnp.broadcast_to(low_y[0, pl.ds(x, 1), :], shape), ydn(hx))
            hz_y = jnp.where(first_row, jnp.broadcast_to(low_y[1, pl.ds(x, 1), :], shape), ydn(hz))
            E[0, x] = E[0, x] + cb * ((hz - hz_y) - (hy - zdn(hy)))
            E[1, x] = E[1, x] + cb * ((hx - zdn(hx)) - (hz - hz_low))
            E[2, x] = E[2, x] + cb * ((hy - hy_low) - (hx - hx_y))
            hy_low, hz_low = hy, hz

        for kind in range(6):
            @pl.when(kinds[kind][3])
            def _():
                copy_of(kind, step).wait_send()
        return carry

    lax.fori_loop(0, steps, one_step, 0)
    stores = [pltpu.make_async_copy(E, e_out, store_sem.at[0]), pltpu.make_async_copy(H, h_out, store_sem.at[1])]
    for copy in stores:
        copy.start()
    for copy in stores:
        copy.wait()
    pltpu.make_async_copy(J, j_out, store_sem.at[2]).wait()


def body(nx, ny, e_field, h_field, currents, material, coating, mat_ca, mat_cb, drude, inc_ez, inc_hy, box):
    _, wx, wy, depth = e_field.shape
    steps = inc_ez.shape[0]
    hbm, smem = pl.BlockSpec(memory_space=pl.ANY), pl.BlockSpec(memory_space=pltpu.SMEM)
    field = pltpu.VMEM((3, wx, wy, depth), jnp.float32)
    cell = pltpu.VMEM((wx, wy, depth), jnp.float32)
    cell_int = pltpu.VMEM((wx, wy, depth), jnp.int32)
    x_plane = pltpu.VMEM((steps, 2, wy, depth), jnp.float32)
    y_plane = pltpu.VMEM((steps, 2, wx, depth), jnp.float32)
    corner = pltpu.VMEM((steps, 1, depth), jnp.float32)
    messages = [x_plane, y_plane, x_plane, y_plane, corner, corner]
    return pl.pallas_call(
        functools.partial(kernel, nx, ny),
        out_shape=[jax.ShapeDtypeStruct(e_field.shape, jnp.float32)] * 3,
        in_specs=[hbm] * 5 + [smem] * 6,
        out_specs=[hbm] * 3,
        scratch_shapes=[field, field, field, cell_int, cell_int, cell, cell]
        + messages + messages + [pltpu.VMEM((2, wx, depth), jnp.float32)]
        + [pltpu.SemaphoreType.DMA((5,)), pltpu.SemaphoreType.DMA((3,)),
           pltpu.SemaphoreType.DMA((steps, 6)), pltpu.SemaphoreType.DMA((steps, 6))],
        compiler_params=pltpu.CompilerParams(collective_id=0, has_side_effects=True),
    )(e_field, h_field, currents, material, coating, mat_ca, mat_cb, drude, inc_ez, inc_hy, box)


def solution(mesh):
    field, cell = P(None, "gx", "gy", None), P("gx", "gy", None)
    return jax.shard_map(
        functools.partial(body, mesh.shape["gx"], mesh.shape["gy"]),
        mesh=mesh,
        in_specs=(field, field, field, cell, cell, P(), P(), P(), P(), P(), P()),
        out_specs=(field, field, field),
        check_vma=False,
    )
```

```python
import functools

import jax
import jax.numpy as jnp
from jax import lax
from jax.experimental import pallas as pl
from jax.experimental.pallas import tpu as pltpu
from jax.sharding import PartitionSpec as P

CH = 0.5
MESH = pl.DeviceIdType.MESH

EX, EY, HX, HY, CEY, CEX = range(6)


def kernel(nx, ny, e_in, h_in, j_in, mat_in, coat_in, ca_in, cb_in, drude_in, ez_in, hy_in, box_in,
           E, H, J, M, C, CA, CB, mat_ca, mat_cb, drude, inc_ez, inc_hy, box,
           s_ex, s_ey, s_hx, s_hy, s_cey, s_cex, r_ex, r_ey, r_hx, r_hy, r_cey, r_cex, low_y,
           load_sem, send_sem, recv_sem):
    gx, gy = lax.axis_index("gx"), lax.axis_index("gy")
    steps = inc_ez.shape[0]
    wx, wy, depth = M.shape
    line_len = inc_ez.shape[1]

    loads = [pltpu.make_async_copy(src, dst, load_sem.at[i])
             for i, (src, dst) in enumerate([
                 (ca_in, mat_ca), (cb_in, mat_cb), (drude_in, drude), (ez_in, inc_ez), (hy_in, inc_hy),
                 (box_in, box), (mat_in, M), (coat_in, C), (e_in, E), (h_in, H), (j_in, J)])]
    for copy in loads:
        copy.start()

    has_lx, has_ux, has_ly, has_uy = gx > 0, gx < nx - 1, gy > 0, gy < ny - 1
    down_up, up_down = has_lx & has_uy, has_ux & has_ly
    to_lx, to_ux = (gx - 1, gy), (gx + 1, gy)
    to_ly, to_uy = (gx, gy - 1), (gx, gy + 1)
    to_du, to_ud = (gx - 1, gy + 1), (gx + 1, gy - 1)
    kinds = [
        (s_ex, r_ex, to_lx, has_lx, has_ux),
        (s_ey, r_ey, to_ly, has_ly, has_uy),
        (s_hx, r_hx, to_ux, has_ux, has_lx),
        (s_hy, r_hy, to_uy, has_uy, has_ly),
        (s_cey, r_cey, to_du, down_up, up_down),
        (s_cex, r_cex, to_ud, up_down, down_up),
    ]

    for _, dst, _, _, comes in kinds:
        @pl.when(jnp.logical_not(comes))
        def _():
            dst[...] = jnp.zeros_like(dst)

    barrier = pltpu.get_barrier_semaphore()
    for target, exists in [(to_lx, has_lx), (to_ux, has_ux), (to_ly, has_ly), (to_uy, has_uy),
                           (to_du, down_up), (to_ud, up_down)]:
        @pl.when(exists)
        def _():
            pl.semaphore_signal(barrier, inc=1, device_id=target, device_id_type=MESH)

    def copy_of(kind, step):
        src, dst, target, _, _ = kinds[kind]
        return pltpu.make_async_remote_copy(
            src_ref=src.at[step], dst_ref=dst.at[step], send_sem=send_sem.at[step, kind],
            recv_sem=recv_sem.at[step, kind], device_id=target, device_id_type=MESH)

    def send(kind, step):
        @pl.when(kinds[kind][3])
        def _():
            copy_of(kind, step).start()

    for copy in loads[:7]:
        copy.wait()
    x0, x1, y0, y1, z0, z1 = [box[i] for i in range(6)]
    shape = (wy, depth)
    row = lax.broadcasted_iota(jnp.int32, shape, 0)
    lane = lax.broadcasted_iota(jnp.int32, shape, 1)
    yi = row + gy * wy
    first_row, last_row = row == 0, row == wy - 1
    first_lane, last_lane = lane == 0, lane == depth - 1
    in_y = (yi >= y0) & (yi <= y1)
    in_z = (lane >= z0) & (lane <= z1)
    f32 = lambda cond: jnp.where(cond, 1.0, 0.0).astype(jnp.float32)
    zero = jnp.zeros(shape, jnp.float32)
    w_yz = f32(in_y & in_z)
    fy_z = (f32(yi == y0 - 1) - f32(yi == y1)) * f32(in_z) * CH
    y_fz = f32(in_y) * (f32(lane == z0) - f32(lane == z1))
    start_x = gx * wx

    zup = lambda f: jnp.where(last_lane, zero, pltpu.roll(f, depth - 1, 1))
    zdn = lambda f: jnp.where(first_lane, zero, pltpu.roll(f, 1, 1))
    yup = lambda f: pltpu.roll(f, wy - 1, 0)
    ydn = lambda f: pltpu.roll(f, 1, 0)

    a = [mat_ca[i] for i in range(mat_ca.shape[0])]
    b = [mat_cb[i] for i in range(mat_cb.shape[0])]
    for x in range(wx):
        m = M[x]
        va, vb = jnp.full(shape, a[0], jnp.float32), jnp.full(shape, b[0], jnp.float32)
        for i in range(1, len(a)):
            va, vb = jnp.where(m == i, a[i], va), jnp.where(m == i, b[i], vb)
        CA[x], CB[x] = va, vb
    kd, bd = drude[0], drude[1]
    for copy in loads[7:]:
        copy.wait()
    pl.semaphore_wait(barrier, sum(jnp.where(c, 1, 0) for c in (has_lx, has_ux, has_ly, has_uy, down_up, up_down)))

    def one_step(step, carry):
        s_ex[step, 0], s_ex[step, 1] = E[1, 0], E[2, 0]
        send(EX, step)
        for x in range(wx):
            s_ey[step, 0, pl.ds(x, 1), :] = E[0, x, pl.ds(0, 1), :]
            s_ey[step, 1, pl.ds(x, 1), :] = E[2, x, pl.ds(0, 1), :]
        send(EY, step)
        s_cey[step] = E[1, 0, pl.ds(wy - 1, 1), :]
        send(CEY, step)
        s_cex[step] = E[0, wx - 1, pl.ds(0, 1), :]
        send(CEX, step)

        ez_x0, ez_x1 = inc_ez[step, x0], inc_ez[step, x1]
        for x in range(wx):
            xi = start_x + x
            ex, ey, ez = E[0, x], E[1, x], E[2, x]
            ey_up = E[1, x + 1] if x + 1 < wx else zero
            ez_up = E[2, x + 1] if x + 1 < wx else zero
            ez_y = jnp.where(last_row, zero, yup(ez))
            ex_y = jnp.where(last_row, zero, yup(ex))
            fx = CH * (jnp.where(xi == x1, ez_x1, 0.0) - jnp.where(xi == x0 - 1, ez_x0, 0.0))
            local = jnp.where((xi >= x0) & (xi <= x1), inc_ez[step, xi], 0.0)
            hx = H[0, x] + CH * ((zup(ey) - ey) - (ez_y - ez)) + local * fy_z
            hy = H[1, x] + CH * ((ez_up - ez) - (zup(ex) - ex)) + fx * w_yz
            hz = H[2, x] + CH * ((ex_y - ex) - (ey_up - ey))
            H[0, x], H[1, x], H[2, x] = hx, hy, hz
            s_hy[step, 0, pl.ds(x, 1), :] = hx[wy - 1:wy]
            s_hy[step, 1, pl.ds(x, 1), :] = hz[wy - 1:wy]
        send(HY, step)
        s_hx[step, 0], s_hx[step, 1] = H[1, wx - 1], H[2, wx - 1]
        send(HX, step)

        hy_x0, hy_x1 = inc_hy[step, jnp.maximum(x0 - 1, 0)], inc_hy[step, x1]
        for x in range(wx):
            xi = start_x + x
            fx = jnp.where(xi == x1, hy_x1, 0.0) - jnp.where(xi == x0, hy_x0, 0.0)
            local = jnp.where((xi >= x0) & (xi < x1), inc_hy[step, xi], 0.0)
            coat = C[x] == 1
            ca, cb = CA[x], CB[x]
            for c in range(3):
                e = E[c, x]
                j = jnp.where(coat, kd * J[c, x] + bd * e, zero)
                J[c, x] = j
                t = -j
                if c == 0:
                    t = local * y_fz - j
                if c == 2:
                    t = fx * w_yz - j
                E[c, x] = ca * e + cb * t

        for kind in range(6):
            @pl.when(kinds[kind][4])
            def _():
                copy_of(kind, step).wait_recv()

        has_y = jnp.where(has_ly, 1.0, 0.0).astype(jnp.float32)
        has_x = jnp.where(has_lx, 1.0, 0.0).astype(jnp.float32)
        low_y[0] = has_y * (r_hy[step, 0] - CH * s_ey[step, 1])
        low_y[1] = has_y * (r_hy[step, 1] + CH * s_ey[step, 0])
        low_y[1, pl.ds(wx - 1, 1), :] = low_y[1, pl.ds(wx - 1, 1), :] - (CH * has_y) * r_cey[step]
        hy_low = has_x * (r_hx[step, 0] + CH * s_ex[step, 1])
        corner = jnp.where(last_row, jnp.broadcast_to(r_cex[step], shape), zero)
        hz_low = has_x * (r_hx[step, 1] - CH * (s_ex[step, 0] - corner))
        for x in range(wx):
            ez_up = jnp.broadcast_to(r_ey[step, 1, pl.ds(x, 1), :], shape)
            ex_up = jnp.broadcast_to(r_ey[step, 0, pl.ds(x, 1), :], shape)
            hx = H[0, x] - jnp.where(last_row, CH * ez_up, zero)
            hy = H[1, x]
            hz = H[2, x] + jnp.where(last_row, CH * ex_up, zero)
            if x == wx - 1:
                hy = hy + CH * r_ex[step, 1]
                hz = hz - CH * r_ex[step, 0]
                H[1, x] = hy
            H[0, x], H[2, x] = hx, hz
            cb = CB[x]
            hx_y = jnp.where(first_row, jnp.broadcast_to(low_y[0, pl.ds(x, 1), :], shape), ydn(hx))
            hz_y = jnp.where(first_row, jnp.broadcast_to(low_y[1, pl.ds(x, 1), :], shape), ydn(hz))
            E[0, x] = E[0, x] + cb * ((hz - hz_y) - (hy - zdn(hy)))
            E[1, x] = E[1, x] + cb * ((hx - zdn(hx)) - (hz - hz_low))
            E[2, x] = E[2, x] + cb * ((hy - hy_low) - (hx - hx_y))
            hy_low, hz_low = hy, hz

        for kind in range(6):
            @pl.when(kinds[kind][3])
            def _():
                copy_of(kind, step).wait_send()
        return carry

    lax.fori_loop(0, steps, one_step, 0)


def write_out(*refs):
    *ends, sems = refs
    count = len(ends) // 2
    copies = [pltpu.make_async_copy(src, dst, sems.at[i])
              for i, (src, dst) in enumerate(zip(ends[:count], ends[count:]))]
    for copy in copies:
        copy.start()
    for copy in copies:
        copy.wait()


def body(nx, ny, e_field, h_field, currents, material, coating, mat_ca, mat_cb, drude, inc_ez, inc_hy, box):
    _, wx, wy, depth = e_field.shape
    steps = inc_ez.shape[0]
    hbm = pl.BlockSpec(memory_space=pltpu.HBM)
    vmem = pl.BlockSpec(memory_space=pltpu.VMEM)
    cell = pltpu.VMEM((wx, wy, depth), jnp.float32)
    cell_int = pltpu.VMEM((wx, wy, depth), jnp.int32)
    x_plane = pltpu.VMEM((steps, 2, wy, depth), jnp.float32)
    y_plane = pltpu.VMEM((steps, 2, wx, depth), jnp.float32)
    corner = pltpu.VMEM((steps, 1, depth), jnp.float32)
    messages = [x_plane, y_plane, x_plane, y_plane, corner, corner]
    small = (mat_ca, mat_cb, drude, inc_ez, inc_hy, box)
    fields = pl.pallas_call(
        functools.partial(kernel, nx, ny),
        out_shape=[pltpu.VMEM(e_field.shape, jnp.float32)] * 3,
        in_specs=[hbm] * 11,
        out_specs=[vmem] * 3,
        scratch_shapes=[cell_int, cell_int, cell, cell] + [pltpu.SMEM(a.shape, a.dtype) for a in small]
        + messages + messages + [pltpu.VMEM((2, wx, depth), jnp.float32)]
        + [pltpu.SemaphoreType.DMA((11,)),
           pltpu.SemaphoreType.DMA((steps, 6)), pltpu.SemaphoreType.DMA((steps, 6))],
        compiler_params=pltpu.CompilerParams(
            collective_id=0, has_side_effects=True, vmem_limit_bytes=int(60 * 2**20)),
    )(e_field, h_field, currents, material, coating, *small)
    return pl.pallas_call(
        write_out,
        out_shape=[jax.ShapeDtypeStruct(e_field.shape, jnp.float32)] * 3,
        in_specs=[vmem] * 3,
        out_specs=[hbm] * 3,
        scratch_shapes=[pltpu.SemaphoreType.DMA((3,))],
        compiler_params=pltpu.CompilerParams(vmem_limit_bytes=8 * 2**20),
    )(*fields)


def solution(mesh):
    field, cell = P(None, "gx", "gy", None), P("gx", "gy", None)
    return jax.shard_map(
        functools.partial(body, mesh.shape["gx"], mesh.shape["gy"]),
        mesh=mesh,
        in_specs=(field, field, field, cell, cell, P(), P(), P(), P(), P(), P()),
        out_specs=(field, field, field),
        check_vma=False,
    )
```

```python
import functools

import jax
import jax.numpy as jnp
from jax import lax
from jax.experimental import pallas as pl
from jax.experimental.pallas import tpu as pltpu
from jax.sharding import PartitionSpec as P

CH = 0.5
MESH = pl.DeviceIdType.MESH

EX, EY, HX, HY, CEY, CEX = range(6)


def kernel(nx, ny, e_in, h_in, j_in, mat_in, coat_in, ca_in, cb_in, drude_in, ez_in, hy_in, box_in,
           E, H, J, M, C, CA, CB, mat_ca, mat_cb, drude, inc_ez, inc_hy, box,
           s_ex, s_ey, s_hx, s_hy, s_cey, s_cex, r_ex, r_ey, r_hx, r_hy, r_cey, r_cex, low_y,
           load_sem, send_sem, recv_sem):
    gx, gy = lax.axis_index("gx"), lax.axis_index("gy")
    steps = inc_ez.shape[0]
    wx, wy, depth = M.shape
    line_len = inc_ez.shape[1]

    has_lx, has_ux, has_ly, has_uy = gx > 0, gx < nx - 1, gy > 0, gy < ny - 1
    down_up, up_down = has_lx & has_uy, has_ux & has_ly
    to_lx, to_ux = (gx - 1, gy), (gx + 1, gy)
    to_ly, to_uy = (gx, gy - 1), (gx, gy + 1)
    to_du, to_ud = (gx - 1, gy + 1), (gx + 1, gy - 1)
    kinds = [
        (s_ex, r_ex, to_lx, has_lx, has_ux),
        (s_ey, r_ey, to_ly, has_ly, has_uy),
        (s_hx, r_hx, to_ux, has_ux, has_lx),
        (s_hy, r_hy, to_uy, has_uy, has_ly),
        (s_cey, r_cey, to_du, down_up, up_down),
        (s_cex, r_cex, to_ud, up_down, down_up),
    ]

    barrier = pltpu.get_barrier_semaphore()
    for target, exists in [(to_lx, has_lx), (to_ux, has_ux), (to_ly, has_ly), (to_uy, has_uy),
                           (to_du, down_up), (to_ud, up_down)]:
        @pl.when(exists)
        def _():
            pl.semaphore_signal(barrier, inc=1, device_id=target, device_id_type=MESH)

    loads = [pltpu.make_async_copy(src, dst, load_sem.at[i])
             for i, (src, dst) in enumerate([
                 (ca_in, mat_ca), (cb_in, mat_cb), (drude_in, drude), (ez_in, inc_ez), (hy_in, inc_hy),
                 (box_in, box), (mat_in, M), (coat_in, C), (e_in, E), (h_in, H), (j_in, J)])]
    for copy in loads:
        copy.start()

    for _, dst, _, _, comes in kinds:
        @pl.when(jnp.logical_not(comes))
        def _():
            dst[...] = jnp.zeros_like(dst)

    def copy_of(kind, step):
        src, dst, target, _, _ = kinds[kind]
        return pltpu.make_async_remote_copy(
            src_ref=src.at[step], dst_ref=dst.at[step], send_sem=send_sem.at[step, kind],
            recv_sem=recv_sem.at[step, kind], device_id=target, device_id_type=MESH)

    def send(kind, step):
        @pl.when(kinds[kind][3])
        def _():
            copy_of(kind, step).start()

    for copy in loads[:7]:
        copy.wait()
    x0, x1, y0, y1, z0, z1 = [box[i] for i in range(6)]
    shape = (wy, depth)
    row = lax.broadcasted_iota(jnp.int32, shape, 0)
    lane = lax.broadcasted_iota(jnp.int32, shape, 1)
    yi = row + gy * wy
    first_row, last_row = row == 0, row == wy - 1
    first_lane, last_lane = lane == 0, lane == depth - 1
    in_y = (yi >= y0) & (yi <= y1)
    in_z = (lane >= z0) & (lane <= z1)
    f32 = lambda cond: jnp.where(cond, 1.0, 0.0).astype(jnp.float32)
    zero = jnp.zeros(shape, jnp.float32)
    w_yz = f32(in_y & in_z)
    fy_z = (f32(yi == y0 - 1) - f32(yi == y1)) * f32(in_z) * CH
    y_fz = f32(in_y) * (f32(lane == z0) - f32(lane == z1))
    start_x = gx * wx

    zup = lambda f: jnp.where(last_lane, zero, pltpu.roll(f, depth - 1, 1))
    zdn = lambda f: jnp.where(first_lane, zero, pltpu.roll(f, 1, 1))
    yup = lambda f: pltpu.roll(f, wy - 1, 0)
    ydn = lambda f: pltpu.roll(f, 1, 0)

    a = [mat_ca[i] for i in range(mat_ca.shape[0])]
    b = [mat_cb[i] for i in range(mat_cb.shape[0])]
    for x in range(wx):
        m = M[x]
        va, vb = jnp.full(shape, a[0], jnp.float32), jnp.full(shape, b[0], jnp.float32)
        for i in range(1, len(a)):
            va, vb = jnp.where(m == i, a[i], va), jnp.where(m == i, b[i], vb)
        CA[x], CB[x] = va, vb
    kd, bd = drude[0], drude[1]
    for copy in loads[7:]:
        copy.wait()
    pl.semaphore_wait(barrier, sum(jnp.where(c, 1, 0) for c in (has_lx, has_ux, has_ly, has_uy, down_up, up_down)))

    def stage_rows(step, x, ex, ez):
        s_ey[step, 0, pl.ds(x, 1), :] = ex[:1]
        s_ey[step, 1, pl.ds(x, 1), :] = ez[:1]

    for x in range(wx):
        stage_rows(0, x, E[0, x], E[2, x])

    def one_step(step, carry):
        s_cey[step] = E[1, 0, pl.ds(wy - 1, 1), :]
        send(CEY, step)
        s_cex[step] = E[0, wx - 1, pl.ds(0, 1), :]
        send(CEX, step)
        send(EY, step)
        s_ex[step, 0], s_ex[step, 1] = E[1, 0], E[2, 0]
        send(EX, step)

        ez_x0, ez_x1 = inc_ez[step, x0], inc_ez[step, x1]
        for x in range(wx):
            xi = start_x + x
            ex, ey, ez = E[0, x], E[1, x], E[2, x]
            ey_up = E[1, x + 1] if x + 1 < wx else zero
            ez_y = jnp.where(last_row, zero, yup(ez))
            ex_y = jnp.where(last_row, zero, yup(ex))
            local = jnp.where((xi >= x0) & (xi <= x1), inc_ez[step, xi], 0.0)
            hx = H[0, x] + CH * ((zup(ey) - ey) - (ez_y - ez)) + local * fy_z
            hz = H[2, x] + CH * ((ex_y - ex) - (ey_up - ey))
            H[0, x], H[2, x] = hx, hz
            s_hy[step, 0, pl.ds(x, 1), :] = hx[wy - 1:wy]
            s_hy[step, 1, pl.ds(x, 1), :] = hz[wy - 1:wy]
        send(HY, step)

        def update_hy(x):
            xi = start_x + x
            ex, ez = E[0, x], E[2, x]
            ez_up = E[2, x + 1] if x + 1 < wx else zero
            fx = CH * (jnp.where(xi == x1, ez_x1, 0.0) - jnp.where(xi == x0 - 1, ez_x0, 0.0))
            H[1, x] = H[1, x] + CH * ((ez_up - ez) - (zup(ex) - ex)) + fx * w_yz

        update_hy(wx - 1)
        s_hx[step, 0], s_hx[step, 1] = H[1, wx - 1], H[2, wx - 1]
        send(HX, step)

        hy_x0, hy_x1 = inc_hy[step, jnp.maximum(x0 - 1, 0)], inc_hy[step, x1]
        for x in range(wx):
            if x < wx - 1:
                update_hy(x)
            xi = start_x + x
            fx = jnp.where(xi == x1, hy_x1, 0.0) - jnp.where(xi == x0, hy_x0, 0.0)
            local = jnp.where((xi >= x0) & (xi < x1), inc_hy[step, xi], 0.0)
            coat = C[x] == 1
            ca, cb = CA[x], CB[x]
            for c in range(3):
                e = E[c, x]
                j = jnp.where(coat, kd * J[c, x] + bd * e, zero)
                J[c, x] = j
                t = -j
                if c == 0:
                    t = local * y_fz - j
                if c == 2:
                    t = fx * w_yz - j
                E[c, x] = ca * e + cb * t

        for kind in range(6):
            @pl.when(kinds[kind][3])
            def _():
                copy_of(kind, step).wait_send()
        def receive(*which):
            for kind in which:
                @pl.when(kinds[kind][4])
                def _():
                    copy_of(kind, step).wait_recv()

        receive(EX, HX, EY, HY)

        has_y = jnp.where(has_ly, 1.0, 0.0).astype(jnp.float32)
        has_x = jnp.where(has_lx, 1.0, 0.0).astype(jnp.float32)
        low_y[0] = has_y * (r_hy[step, 0] - CH * s_ey[step, 1])
        low_y[1] = has_y * (r_hy[step, 1] + CH * s_ey[step, 0])
        hy_low = has_x * (r_hx[step, 0] + CH * s_ex[step, 1])
        hz_low = has_x * (r_hx[step, 1] - CH * s_ex[step, 0])
        for x in range(wx):
            ez_up = jnp.broadcast_to(r_ey[step, 1, pl.ds(x, 1), :], shape)
            ex_up = jnp.broadcast_to(r_ey[step, 0, pl.ds(x, 1), :], shape)
            hx = H[0, x] - jnp.where(last_row, CH * ez_up, zero)
            hy = H[1, x]
            hz = H[2, x] + jnp.where(last_row, CH * ex_up, zero)
            if x == wx - 1:
                hy = hy + CH * r_ex[step, 1]
                hz = hz - CH * r_ex[step, 0]
                H[1, x] = hy
            H[0, x], H[2, x] = hx, hz
            cb = CB[x]
            hx_y = jnp.where(first_row, jnp.broadcast_to(low_y[0, pl.ds(x, 1), :], shape), ydn(hx))
            hz_y = jnp.where(first_row, jnp.broadcast_to(low_y[1, pl.ds(x, 1), :], shape), ydn(hz))
            ex = E[0, x] + cb * ((hz - hz_y) - (hy - zdn(hy)))
            ez = E[2, x] + cb * ((hy - hy_low) - (hx - hx_y))
            E[0, x], E[2, x] = ex, ez
            E[1, x] = E[1, x] + cb * ((hx - zdn(hx)) - (hz - hz_low))
            stage_rows(step + 1, x, ex, ez)
            hy_low, hz_low = hy, hz

        receive(CEY, CEX)
        top, end = pl.ds(0, 1), pl.ds(wy - 1, 1)
        line = E[0, wx - 1, top, :] + CB[wx - 1, top, :] * ((CH * has_y) * r_cey[step])
        E[0, wx - 1, top, :] = line
        s_ey[step + 1, 0, pl.ds(wx - 1, 1), :] = line
        E[1, 0, end, :] = E[1, 0, end, :] + CB[0, end, :] * ((CH * has_x) * r_cex[step])

        return carry

    lax.fori_loop(0, steps, one_step, 0)


def write_out(*refs):
    *ends, sems = refs
    count = len(ends) // 2
    copies = [pltpu.make_async_copy(src, dst, sems.at[i])
              for i, (src, dst) in enumerate(zip(ends[:count], ends[count:]))]
    for copy in copies:
        copy.start()
    for copy in copies:
        copy.wait()


def body(nx, ny, e_field, h_field, currents, material, coating, mat_ca, mat_cb, drude, inc_ez, inc_hy, box):
    _, wx, wy, depth = e_field.shape
    steps = inc_ez.shape[0]
    hbm = pl.BlockSpec(memory_space=pltpu.HBM)
    vmem = pl.BlockSpec(memory_space=pltpu.VMEM)
    cell = pltpu.VMEM((wx, wy, depth), jnp.float32)
    cell_int = pltpu.VMEM((wx, wy, depth), jnp.int32)
    x_plane = pltpu.VMEM((steps, 2, wy, depth), jnp.float32)
    y_plane = pltpu.VMEM((steps, 2, wx, depth), jnp.float32)
    corner = pltpu.VMEM((steps, 1, depth), jnp.float32)
    messages = [x_plane, y_plane, x_plane, y_plane, corner, corner]
    sent = [x_plane, pltpu.VMEM((steps + 1, 2, wx, depth), jnp.float32)] + messages[2:]
    small = (mat_ca, mat_cb, drude, inc_ez, inc_hy, box)
    fields = pl.pallas_call(
        functools.partial(kernel, nx, ny),
        out_shape=[pltpu.VMEM(e_field.shape, jnp.float32)] * 3,
        in_specs=[hbm] * 11,
        out_specs=[vmem] * 3,
        scratch_shapes=[cell_int, cell_int, cell, cell] + [pltpu.SMEM(a.shape, a.dtype) for a in small]
        + sent + messages + [pltpu.VMEM((2, wx, depth), jnp.float32)]
        + [pltpu.SemaphoreType.DMA((11,)),
           pltpu.SemaphoreType.DMA((steps, 6)), pltpu.SemaphoreType.DMA((steps, 6))],
        compiler_params=pltpu.CompilerParams(
            collective_id=0, has_side_effects=True, vmem_limit_bytes=int(60 * 2**20)),
    )(e_field, h_field, currents, material, coating, *small)
    return pl.pallas_call(
        write_out,
        out_shape=[jax.ShapeDtypeStruct(e_field.shape, jnp.float32)] * 3,
        in_specs=[vmem] * 3,
        out_specs=[hbm] * 3,
        scratch_shapes=[pltpu.SemaphoreType.DMA((3,))],
        compiler_params=pltpu.CompilerParams(vmem_limit_bytes=8 * 2**20),
    )(*fields)


def solution(mesh):
    field, cell = P(None, "gx", "gy", None), P("gx", "gy", None)
    return jax.shard_map(
        functools.partial(body, mesh.shape["gx"], mesh.shape["gy"]),
        mesh=mesh,
        in_specs=(field, field, field, cell, cell, P(), P(), P(), P(), P(), P()),
        out_specs=(field, field, field),
        check_vma=False,
    )
```
